32 devices in a mesh: segment: 16 (over z, y, core), rows: 2 (over x).
Axes of the slice: x: 2, y: 2, z: 4, core: 2. Of those that a mesh axis runs over, the one named last changes fastest.
Arguments:
- encoder_weight: bfloat16 [16, 3, 3, 384, 384], P('segment', None, None, 'rows'), may hold values from -0.109375 to 0.109375
- encoder_bias: float32 [16, 384], P('segment'), may hold values from -3 to 3
- decoder_weight: bfloat16 [16, 3, 3, 768, 384], P('segment', None, None, 'rows'), may hold values from -0.078125 to 0.078125
- decoder_bias: float32 [16, 384], P('segment'), may hold values from -3 to 3
- encoder_inputs: bfloat16 [16, 1, 6, 64, 384], P('segment', None, 'rows'), may hold values from -6 to 6
- decoder_inputs: bfloat16 [16, 1, 6, 64, 384], P('segment', None, 'rows'), may hold values from -6 to 6
- arrivals: bfloat16 [3, 1, 6, 64, 384], P(None, None, 'rows'), may hold values from -6 to 6
- skip_buffer: bfloat16 [16, 4, 1, 6, 64, 384], P('segment', None, None, 'rows'), may hold values from -6 to 6
Outputs:
- encoder_results: bfloat16 [16, 4, 1, 6, 64, 384], P('segment', None, None, 'rows')
- decoder_results: bfloat16 [16, 4, 1, 6, 64, 384], P('segment', None, None, 'rows')
The draws below stay inside these ranges and needn't reach their ends.
All inputs are finite; a program needn't handle non-finite values.
Results may differ from the reference program's by a relative error of at most 0.0036.
Values may be sent and summed in bfloat16 or wider, within the bound.
A program may use at most 64 MiB of HBM per device.

```python
import jax
import jax.numpy as jnp
from jax import lax

C = 384
W = 64
MB = 1
TICKS = 4
H = 6
SEGMENTS = 16


def steps_of(own_key, shape, split, low, top_value):
    level, own = 1.0, jax.random.fold_in(own_key, 6)
    for dim, blocks in split:
        heights = jnp.exp(jax.random.uniform(jax.random.fold_in(own, dim), (blocks,), jnp.float32, low / len(split), top_value / len(split)))
        level = level * jnp.repeat(heights, shape[dim] // blocks).reshape([-1 if axis == dim else 1 for axis in range(len(shape))])
    return level


def bell_draw(stream_key, shape, spread, bound, split=(), kind=jnp.bfloat16):
    array = jax.random.normal(stream_key, shape, jnp.float32) * spread
    if len(split) > 0:
        array = steps_of(stream_key, shape, split, -0.22, 0.18) * array
    return jnp.clip(array, min=-bound, max=bound).astype(kind)


def setup_inputs(seed: int = 0) -> dict:
    arg_keys = jax.random.split(jax.random.key(seed), 9)
    encoder_weight = bell_draw(arg_keys[0], (SEGMENTS, 3, 3, C, C), (9 * C) ** -0.5, 0.109375, ((0, 16), (3, 2)))
    encoder_bias = bell_draw(arg_keys[1], (SEGMENTS, C), 0.5, 3.0, ((0, 16),), jnp.float32)
    decoder_weight = bell_draw(arg_keys[2], (SEGMENTS, 3, 3, 2 * C, C), (18 * C) ** -0.5, 0.078125, ((0, 16), (3, 2)))
    decoder_bias = bell_draw(arg_keys[3], (SEGMENTS, C), 0.5, 3.0, ((0, 16),), jnp.float32)
    encoder_inputs = bell_draw(arg_keys[4], (SEGMENTS, MB, H, W, C), 1.0, 6.0, ((0, 16), (2, 2)))
    decoder_inputs = bell_draw(arg_keys[5], (SEGMENTS, MB, H, W, C), 1.0, 6.0, ((0, 16), (2, 2)))
    arrivals = bell_draw(arg_keys[6], (TICKS - 1, MB, H, W, C), 1.0, 6.0, ((2, 2),))
    skip_buffer = bell_draw(arg_keys[7], (SEGMENTS, TICKS, MB, H, W, C), 1.0, 6.0, ((0, 16), (3, 2)))
    return {"encoder_weight": encoder_weight, "encoder_bias": encoder_bias, "decoder_weight": decoder_weight, "decoder_bias": decoder_bias, "encoder_inputs": encoder_inputs, "decoder_inputs": decoder_inputs, "arrivals": arrivals, "skip_buffer": skip_buffer}


NUMBERS = ("NHWC", "HWIO", "NHWC")


def segment_layer(source, kernel, offset):
    result = lax.conv_general_dilated(source.astype(jnp.float32), kernel.astype(jnp.float32), (1, 1), ((1, 1), (1, 1)), dimension_numbers=NUMBERS, precision=lax.Precision.HIGHEST)
    return jax.nn.silu(result + offset).astype(jnp.bfloat16)


def reference(encoder_weight, encoder_bias, decoder_weight, decoder_bias, encoder_inputs, decoder_inputs, arrivals, skip_buffer):
    layered = jax.vmap(segment_layer)
    skip_lag = 2 * (SEGMENTS - jnp.arange(SEGMENTS, dtype=jnp.int32)) - 1
    encoder_now = encoder_inputs
    decoder_now = decoder_inputs
    encoder_made = []
    decoder_made = []
    for period in range(TICKS):
        skip_now = skip_buffer[:, period]
        for earlier in range(period):
            chosen = (skip_lag == period - earlier)[:, None, None, None, None]
            skip_now = jnp.where(chosen, encoder_made[earlier], skip_now)
        encoder_result = layered(encoder_now, encoder_weight, encoder_bias)
        decoder_result = layered(jnp.concatenate([decoder_now, skip_now], axis=4), decoder_weight, decoder_bias)
        encoder_made.append(encoder_result)
        decoder_made.append(decoder_result)
        if period + 1 < TICKS:
            encoder_now = jnp.concatenate([arrivals[period][None], encoder_result[:-1]], axis=0)
            decoder_now = jnp.concatenate([decoder_result[1:], encoder_result[-1:]], axis=0)
    return jnp.stack(encoder_made, axis=1), jnp.stack(decoder_made, axis=1)
```

```python
import functools

import jax
import jax.numpy as jnp
from jax import lax
from jax.experimental import pallas as pl
from jax.experimental.pallas import tpu as pltpu
from jax.sharding import PartitionSpec as P

NUMBERS = ("NHWC", "HWIO", "NHWC")


def padded(value, sides, width):
    for axis, dim in sides:
        peers, length = (lax.axis_size(axis), value.shape[dim])
        up = [(i, (i + 1) % peers) for i in range(peers - 1)]
        down = [(j, i) for i, j in up]
        last = lax.slice_in_dim(value, length - width, length, axis=dim)
        initial = lax.slice_in_dim(value, 0, width, axis=dim)
        before = lax.ppermute(last, axis, up)
        after = lax.ppermute(initial, axis, down)
        value = jnp.concatenate([before, value, after], axis=dim)
    return value


def shifted(block, axis, distance):
    devices = range(lax.axis_size(axis))
    route = [(i - distance, i) for i in devices if i - distance in devices]
    return lax.ppermute(block, axis, route)


def channel_part(source, kernel):
    return lax.conv_general_dilated(
        source,
        kernel,
        (1, 1),
        ((0, 0), (1, 1)),
        dimension_numbers=NUMBERS,
        preferred_element_type=jnp.float32,
    )


def finish(result, offset, rim_after, first_row, total_rows):
    result = jax.nn.silu(result + offset)
    if rim_after > 0:
        global_row = first_row - rim_after + jnp.arange(result.shape[1])
        inside = (global_row >= 0) & (global_row < total_rows)
        result = jnp.where(inside[None, :, None, None], result, 0.0)
    return result.astype(jnp.bfloat16)


def trim_rows(source, have_rim, want_rim):
    excess = have_rim - want_rim
    if excess == 0:
        return source
    return source[:, excess : source.shape[1] - excess]


MESH = pl.DeviceIdType.MESH
SENT = jnp.bfloat16
TOP = 32768.0


def relay_kernel(
    segments,
    enc_w,
    enc_b,
    dec_w,
    dec_b,
    enc_in,
    dec_in,
    arrivals,
    skips,
    enc_out,
    dec_out,
    kernel,
    skip_kernel,
    held,
    made,
    skip_full,
    partial,
    scale,
    columns,
    total,
    local_sem,
    link_send,
    link_recv,
    relay_send,
    relay_recv,
):
    s = lax.axis_index("segment")
    r = lax.axis_index("rows")
    ticks, half, width, channels = skips.shape
    rows = 2 * half
    cells = rows * width
    taps = enc_w.shape[0]
    part = enc_w.shape[2]
    last = segments - 1
    is_enc = r == 1
    is_dec = r == 0

    def link(number, src, dst):
        return pltpu.make_async_remote_copy(
            src_ref=src,
            dst_ref=dst,
            send_sem=link_send.at[number],
            recv_sem=link_recv.at[number],
            device_id={"segment": s, "rows": 1 - r},
            device_id_type=MESH,
        )

    def relay(tick, segment, row):
        return pltpu.make_async_remote_copy(
            src_ref=made.at[tick],
            dst_ref=held.at[tick + 1],
            send_sem=relay_send.at[tick],
            recv_sem=relay_recv.at[tick],
            device_id={"segment": segment, "rows": row},
            device_id_type=MESH,
        )

    def local(number, src, dst):
        return pltpu.make_async_copy(src, dst, local_sem.at[number])

    first, final = pl.ds(0, half), pl.ds(half, half)

    skip_link = [link(t, skips.at[t], skip_full.at[t, first]) for t in range(ticks)]
    base = ticks
    input_link = link(base, enc_in, held.at[0, first])
    weight_link = [
        link(base + 1 + d, enc_w.at[d], kernel.at[d, :, pl.ds(0, part)]) for d in range(taps)
    ]
    base = base + 1 + taps
    arrival_link = [
        link(base + t, arrivals.at[t], held.at[t + 1, first]) for t in range(ticks - 1)
    ]
    base = base + ticks - 1
    dec_link = [link(base + t, made.at[t, final], dec_out.at[t]) for t in range(ticks)]
    back_input = link(0, dec_in, held.at[0, final])
    partial_link = [link(1 + t, partial.at[t], partial.at[t]) for t in range(ticks)]
    scale_link = [link(1 + ticks + t, scale.at[t], scale.at[t]) for t in range(ticks)]
    enc_link = [
        link(1 + 2 * ticks + t, made.at[t, first], enc_out.at[t]) for t in range(ticks)
    ]

    barrier = pltpu.get_barrier_semaphore()

    def greet(segment, row):
        pl.semaphore_signal(
            barrier, inc=1, device_id={"segment": segment, "rows": row}, device_id_type=MESH
        )

    greet(s, 1 - r)

    @pl.when(is_enc & (s > 0))
    def _():
        greet(s - 1, 1)

    @pl.when(is_enc & (s < last))
    def _():
        greet(s + 1, 1)

    @pl.when(is_dec & (s > 0))
    def _():
        greet(s - 1, 0)

    @pl.when(is_dec & (s < last))
    def _():
        greet(s + 1, 0)

    within = (s > 0) & (s < last)

    @pl.when(within)
    def _():
        pl.semaphore_wait(barrier, 3)

    @pl.when(jnp.logical_not(within))
    def _():
        pl.semaphore_wait(barrier, 2 if segments > 1 else 1)

    def spread(source):
        value = source.reshape(cells, channels).astype(jnp.float32)
        column = lax.broadcasted_iota(jnp.int32, (cells, channels), 0) % width
        left = jnp.where(column == 0, 0.0, pltpu.roll(value, 1, 0))
        right = jnp.where(column == width - 1, 0.0, pltpu.roll(value, cells - 1, 0))
        body = pl.ds(width, cells)
        columns[body, 0:channels] = left.astype(jnp.bfloat16)
        columns[body, channels : 2 * channels] = source.reshape(cells, channels)
        columns[body, 2 * channels :] = right.astype(jnp.bfloat16)

    def convolve(weights):
        def tap(d, carry):
            start = pl.multiple_of(d * width, width)
            total[...] += jnp.dot(
                columns[pl.ds(start, cells), :],
                weights[d].reshape(3 * channels, channels),
                preferred_element_type=jnp.float32,
            )
            return carry

        total[...] = jnp.zeros_like(total)
        lax.fori_loop(0, taps, tap, 0)

    def skip_part(t, source):
        spread(source)
        convolve(skip_kernel)
        found = total[...]
        top = jnp.maximum(jnp.max(jnp.abs(found), axis=(0, 1), keepdims=True), 1e-25)
        scaled = found * (TOP / top)
        power = scaled * scaled
        power = power * power
        power = power * power
        partial[t] = jnp.where(scaled < 0.0, -power, power).astype(SENT)
        scale[t] = jnp.broadcast_to(top * (1.0 / TOP), scale.shape[1:])
        partial_link[t].start()
        scale_link[t].start()

    def layer(t, value):
        result = value / (1.0 + jnp.exp(-value))
        made[t] = result.astype(jnp.bfloat16).reshape(rows, width, channels)

    edge = jnp.zeros((width, 3 * channels), jnp.bfloat16)
    columns[0:width] = edge
    columns[width + cells :] = edge

    fresh = [
        (t, e, segments - (t - e + 1) // 2)
        for t in range(ticks)
        for e in range(t)
        if (t - e) % 2 == 1 and segments >= (t - e + 1) // 2
    ]

    @pl.when(is_dec)
    def _():
        early = ticks // 2
        for t in range(early):
            skip_link[t].start()
        input_link.start()
        for d in range(taps):
            weight_link[d].start()

        @pl.when(s == 0)
        def _():
            for t in range(ticks - 1):
                arrival_link[t].start()

        for t in range(early, ticks):
            skip_link[t].start()
        mine = local(0, dec_in, held.at[0, first])
        weights = local(1, dec_w, kernel)
        mine.start()
        weights.start()
        mine.wait()
        weights.wait()
        back_input.wait_recv()
        outs = []
        for t in range(ticks):
            if t > 0:
                relay(t - 1, s, 0).wait_recv()
            spread(held[t])
            convolve(kernel)
            scale_link[t].wait_recv()
            partial_link[t].wait_recv()
            power = partial[t].astype(jnp.float32)
            root = jnp.sqrt(jnp.sqrt(jnp.sqrt(jnp.abs(power))))
            value = jnp.where(power < 0.0, -root, root) * scale[t, 0:1, 0:1]
            layer(t, total[...] + value + dec_b[...])
            if t + 1 < ticks:

                @pl.when(s > 0)
                def _():
                    relay(t, s - 1, 0).start()

            dec_link[t].start()
            keep = local(2 + t, made.at[t, first], dec_out.at[t])
            keep.start()
            outs.append(keep)
        for keep in outs:
            keep.wait()
        for t in range(ticks):
            skip_link[t].wait_send()
            dec_link[t].wait_send()
            enc_link[t].wait_recv()
        input_link.wait_send()
        for d in range(taps):
            weight_link[d].wait_send()

        @pl.when(s == 0)
        def _():
            for t in range(ticks - 1):
                arrival_link[t].wait_send()

        @pl.when(s > 0)
        def _():
            for t in range(ticks - 1):
                relay(t, s - 1, 0).wait_send()

    @pl.when(is_enc)
    def _():
        back_input.start()
        own_skips = local(0, skips, skip_full.at[:, final])
        skip_weights = local(1, dec_w, skip_kernel)
        mine = local(2, enc_in, held.at[0, final])
        weights = local(3, enc_w, kernel.at[:, :, pl.ds(part, part)])
        for copy in (skip_weights, own_skips, mine, weights):
            copy.start()
        entering = [local(4 + t, arrivals.at[t], held.at[t + 1, final]) for t in range(ticks - 1)]

        @pl.when(s == 0)
        def _():
            for copy in entering:
                copy.start()

        for copy in (skip_weights, own_skips, mine, weights):
            copy.wait()

        def buffered(t):
            skip_link[t].wait_recv()
            usual = True
            for tick, _, segment in fresh:
                if tick == t:
                    usual = jnp.logical_and(usual, s != segment)
            if usual is True:
                skip_part(t, skip_full[t])
            else:

                @pl.when(usual)
                def _():
                    skip_part(t, skip_full[t])

        early = ticks // 2
        for t in range(early):
            buffered(t)
        input_link.wait_recv()
        for d in range(taps):
            weight_link[d].wait_recv()
        outs = []
        for t in range(ticks):
            if t > 0:

                @pl.when(s > 0)
                def _():
                    relay(t - 1, s, 1).wait_recv()

                @pl.when(s == 0)
                def _():
                    arrival_link[t - 1].wait_recv()
                    entering[t - 1].wait()

            spread(held[t])
            convolve(kernel)
            layer(t, total[...] + enc_b[...])
            if t + 1 < ticks:

                @pl.when(s < last)
                def _():
                    relay(t, s + 1, 1).start()

                @pl.when(s == last)
                def _():
                    relay(t, s, 0).start()

            for tick, earlier, segment in fresh:
                if earlier == t:

                    @pl.when(s == segment)
                    def _():
                        skip_part(tick, made[t])

            enc_link[t].start()
            keep = local(4 + ticks + t, made.at[t, final], enc_out.at[t])
            keep.start()
            outs.append(keep)
            if early + t < ticks:
                buffered(early + t)
        for keep in outs:
            keep.wait()
        back_input.wait_send()
        for t in range(ticks):
            partial_link[t].wait_send()
            scale_link[t].wait_send()
            enc_link[t].wait_send()
            dec_link[t].wait_recv()

        @pl.when(s < last)
        def _():
            for t in range(ticks - 1):
                relay(t, s + 1, 1).wait_send()

        @pl.when(s == last)
        def _():
            for t in range(ticks - 1):
                relay(t, s, 0).wait_send()


def owned_shards(
    encoder_weight,
    encoder_bias,
    decoder_weight,
    decoder_bias,
    encoder_inputs,
    decoder_inputs,
    arrivals,
    skip_buffer,
):
    _, ticks, batch, half, width, channels = skip_buffer.shape
    taps = encoder_weight.shape[1]
    rows, cells = 2 * half, 2 * half * width
    links = 3 * ticks + taps
    anywhere = pl.BlockSpec(memory_space=pl.ANY)
    vector = pl.BlockSpec(memory_space=pltpu.VMEM)
    out = jax.ShapeDtypeStruct((ticks, half, width, channels), jnp.bfloat16)
    image = (rows, width, channels)
    encoder_made, decoder_made = pl.pallas_call(
        functools.partial(relay_kernel, lax.axis_size("segment")),
        out_shape=(out, out),
        in_specs=[anywhere, vector, anywhere, vector, anywhere, anywhere, anywhere, anywhere],
        out_specs=(anywhere, anywhere),
        scratch_shapes=[
            pltpu.VMEM((taps, 3, channels, channels), jnp.bfloat16),
            pltpu.VMEM((taps, 3, channels, channels), jnp.bfloat16),
            pltpu.VMEM((ticks,) + image, jnp.bfloat16),
            pltpu.VMEM((ticks,) + image, jnp.bfloat16),
            pltpu.VMEM((ticks,) + image, jnp.bfloat16),
            pltpu.VMEM((ticks, cells, channels), SENT),
            pltpu.VMEM((ticks, 8, 128), jnp.float32),
            pltpu.VMEM((cells + 2 * width, 3 * channels), jnp.bfloat16),
            pltpu.VMEM((cells, channels), jnp.float32),
            pltpu.SemaphoreType.DMA((4 + 2 * ticks,)),
            pltpu.SemaphoreType.DMA((links,)),
            pltpu.SemaphoreType.DMA((links,)),
            pltpu.SemaphoreType.DMA((ticks,)),
            pltpu.SemaphoreType.DMA((ticks,)),
        ],
        compiler_params=pltpu.CompilerParams(
            collective_id=0, has_side_effects=True, vmem_limit_bytes=40 * 1024 * 1024
        ),
    )(
        encoder_weight[0],
        encoder_bias,
        decoder_weight[0],
        decoder_bias,
        encoder_inputs[0, 0],
        decoder_inputs[0, 0],
        arrivals[:, 0],
        skip_buffer[0, :, 0],
    )
    return encoder_made[None, :, None], decoder_made[None, :, None]


def gathered_shards(
    encoder_weight,
    encoder_bias,
    decoder_weight,
    decoder_bias,
    encoder_inputs,
    decoder_inputs,
    arrivals,
    skip_buffer,
):
    segment_count = lax.axis_size("segment")
    segment_index = lax.axis_index("segment")
    rows_local = encoder_inputs.shape[2]
    total_rows = rows_local * lax.axis_size("rows")
    first_row = lax.axis_index("rows") * rows_local
    channels = encoder_weight.shape[4]
    tick_count = skip_buffer.shape[1]
    skip_lag = 2 * (segment_count - segment_index) - 1
    margin = 2
    paired = decoder_weight.reshape(1, 3, 3, decoder_weight.shape[3] // 2, 2 * channels)
    encoder_offset = encoder_bias[0]
    decoder_offset = decoder_bias[0]
    kernels = [None, None]
    gathered = (
        lax.all_gather(encoder_weight, "rows", axis=3, tiled=True),
        lax.all_gather(paired, "rows", axis=3, tiled=True),
    )
    kernels[0] = gathered[0][0]
    kernels[1] = gathered[1].reshape(3, 3, 2 * channels, channels)
    encoder_now = encoder_inputs[0]
    decoder_now = decoder_inputs[0]
    arrival_state = [(arrivals[number], 0) for number in range(tick_count - 1)]
    skip_state = [(skip_buffer[0, number], 0) for number in range(tick_count)]
    encoder_made = []
    encoder_cores = []
    decoder_cores = []

    def pick_skip(period, want_rim):
        base_skip, base_rim = skip_state[period]
        chosen = trim_rows(base_skip, base_rim, want_rim)
        for earlier in range(period):
            if (period - earlier) % 2 == 1:
                made_value, made_rim = encoder_made[earlier]
                chosen = jnp.where(
                    skip_lag == period - earlier, trim_rows(made_value, made_rim, want_rim), chosen
                )
        return chosen

    for period in range(tick_count):
        position = period % margin
        rim_before = margin - position
        if position == 0:
            skip_now = pick_skip(period, 0)
            pieces = [encoder_now, decoder_now, skip_now]
            pieces = pieces + [arrival_state[period][0], skip_state[period + 1][0]]
            joined = jnp.concatenate(pieces, axis=3)
            rimmed = padded(joined, (("rows", 1),), margin)
            sections = [
                rimmed[..., number * channels : (number + 1) * channels]
                for number in range(len(pieces))
            ]
            encoder_now = sections[0]
            decoder_now = sections[1]
            skip_now = sections[2]
            arrival_state[period] = (sections[3], margin)
            skip_state[period + 1] = (sections[4], margin)
        else:
            skip_now = pick_skip(period, rim_before)
        rim_after = rim_before - 1
        decoder_source = jnp.concatenate([decoder_now, skip_now], axis=3)
        encoder_out = finish(
            channel_part(encoder_now, kernels[0]), encoder_offset, rim_after, first_row, total_rows
        )
        decoder_out = finish(
            channel_part(decoder_source, kernels[1]),
            decoder_offset,
            rim_after,
            first_row,
            total_rows,
        )
        encoder_made.append((encoder_out, rim_after))
        encoder_cores.append(trim_rows(encoder_out, rim_after, 0))
        decoder_cores.append(trim_rows(decoder_out, rim_after, 0))
        if period + 1 < tick_count:
            encoder_moved = shifted(encoder_out, "segment", 1)
            decoder_moved = shifted(decoder_out, "segment", -1)
            arrival, arrival_rim = arrival_state[period]
            encoder_now = jnp.where(
                segment_index == 0, trim_rows(arrival, arrival_rim, rim_after), encoder_moved
            )
            decoder_now = jnp.where(segment_index == segment_count - 1, encoder_out, decoder_moved)
    return (jnp.stack(encoder_cores, axis=0)[None], jnp.stack(decoder_cores, axis=0)[None])


def solution(mesh):
    return jax.shard_map(
        owned_shards if mesh.shape["rows"] == 2 else gathered_shards,
        mesh=mesh,
        in_specs=(
            P("segment", None, None, "rows", None),
            P("segment", None),
            P("segment", None, None, "rows", None),
            P("segment", None),
            P("segment", None, "rows", None, None),
            P("segment", None, "rows", None, None),
            P(None, None, "rows", None, None),
            P("segment", None, None, "rows", None, None),
        ),
        out_specs=(
            P("segment", None, None, "rows", None, None),
            P("segment", None, None, "rows", None, None),
        ),
        check_vma=False,
    )
```

```python
import functools

import jax
import jax.numpy as jnp
from jax import lax
from jax.experimental import pallas as pl
from jax.experimental.pallas import tpu as pltpu
from jax.sharding import PartitionSpec as P

NUMBERS = ("NHWC", "HWIO", "NHWC")


def padded(value, sides, width):
    for axis, dim in sides:
        peers, length = (lax.axis_size(axis), value.shape[dim])
        up = [(i, (i + 1) % peers) for i in range(peers - 1)]
        down = [(j, i) for i, j in up]
        last = lax.slice_in_dim(value, length - width, length, axis=dim)
        initial = lax.slice_in_dim(value, 0, width, axis=dim)
        before = lax.ppermute(last, axis, up)
        after = lax.ppermute(initial, axis, down)
        value = jnp.concatenate([before, value, after], axis=dim)
    return value


def shifted(block, axis, distance):
    devices = range(lax.axis_size(axis))
    route = [(i - distance, i) for i in devices if i - distance in devices]
    return lax.ppermute(block, axis, route)


def channel_part(source, kernel):
    return lax.conv_general_dilated(
        source,
        kernel,
        (1, 1),
        ((0, 0), (1, 1)),
        dimension_numbers=NUMBERS,
        preferred_element_type=jnp.float32,
    )


def finish(result, offset, rim_after, first_row, total_rows):
    result = jax.nn.silu(result + offset)
    if rim_after > 0:
        global_row = first_row - rim_after + jnp.arange(result.shape[1])
        inside = (global_row >= 0) & (global_row < total_rows)
        result = jnp.where(inside[None, :, None, None], result, 0.0)
    return result.astype(jnp.bfloat16)


def trim_rows(source, have_rim, want_rim):
    excess = have_rim - want_rim
    if excess == 0:
        return source
    return source[:, excess : source.shape[1] - excess]


MESH = pl.DeviceIdType.MESH
SENT = jnp.bfloat16
TOP = 32768.0


def coded(found):
    top = jnp.maximum(jnp.max(jnp.abs(found), axis=(0, 1), keepdims=True), 1e-25)
    scaled = found * (TOP / top)
    power = scaled * scaled
    power = power * power
    power = power * power
    return jnp.where(scaled < 0.0, -power, power).astype(SENT), top * (1.0 / TOP)


def decoded(code, scale):
    power = code.astype(jnp.float32)
    root = jnp.sqrt(jnp.sqrt(jnp.sqrt(jnp.abs(power))))
    return jnp.where(power < 0.0, -root, root) * scale


def low_lanes(shape, part):
    return lax.broadcasted_iota(jnp.int32, shape, 1) < part


def packed(value, side):
    count, part = value.shape[0] // 2, value.shape[1] // 2
    upper, lower = value[:count], value[count:]
    left = jnp.where(side == 0, upper, pltpu.roll(upper, part, 1))
    right = jnp.where(side == 0, pltpu.roll(lower, part, 1), lower)
    return jnp.where(low_lanes(upper.shape, part), left, right)


def unpacked(value, side):
    part = value.shape[1] // 2
    turned = pltpu.roll(value, part, 1)
    return jnp.where(side == 0, value, turned), jnp.where(side == 0, turned, value)


def silu(value):
    return value / (1.0 + jnp.exp(-value))


def relay_kernel(
    segments,
    enc_w,
    enc_b,
    dec_w,
    dec_b,
    enc_in,
    dec_in,
    arrivals,
    skips,
    enc_out,
    dec_out,
    wide,
    narrow,
    bias,
    held,
    made,
    skip_full,
    partial,
    scale,
    own_in,
    cut_send,
    cut_recv,
    sum_send,
    sum_recv,
    sum_scale_send,
    sum_scale_recv,
    enc_held,
    enc_made,
    enc_other,
    out_send,
    out_recv,
    enc_final,
    columns,
    total,
    mine,
    flat,
    local_sem,
    link_send,
    link_recv,
    relay_send,
    relay_recv,
):
    s = lax.axis_index("segment")
    r = lax.axis_index("rows")
    ticks, half, width, channels = skips.shape
    rows = 2 * half
    cells = rows * width
    own = half * width
    taps = enc_w.shape[0]
    part = enc_w.shape[2]
    slot = narrow.shape[2]
    last = segments - 1
    is_enc = r == 1
    is_dec = r == 0
    counter = [0]

    def link(src, dst):
        number = counter[0]
        counter[0] = number + 1
        return pltpu.make_async_remote_copy(
            src_ref=src,
            dst_ref=dst,
            send_sem=link_send.at[number],
            recv_sem=link_recv.at[number],
            device_id={"segment": s, "rows": 1 - r},
            device_id_type=MESH,
        )

    def relay(number, src, dst, segment):
        return pltpu.make_async_remote_copy(
            src_ref=src,
            dst_ref=dst,
            send_sem=relay_send.at[number],
            recv_sem=relay_recv.at[number],
            device_id={"segment": segment, "rows": r},
            device_id_type=MESH,
        )

    def local(src, dst):
        number = counter[0]
        counter[0] = number + 1
        return pltpu.make_async_copy(src, dst, local_sem.at[number])

    def enc_relay(t):
        return relay(t, enc_made.at[t], enc_held.at[t + 1], s + 1)

    def dec_relay(t):
        return relay(ticks + t, made.at[t], held.at[t + 1], s - 1)

    first, final = pl.ds(0, half), pl.ds(half, half)

    cut_link = [link(cut_send.at[t], cut_recv.at[t]) for t in range(ticks)]
    sum_link = [link(sum_send.at[t], sum_recv.at[t]) for t in range(ticks)]
    sum_scale_link = [link(sum_scale_send.at[t], sum_scale_recv.at[t]) for t in range(ticks)]
    out_link = [link(out_send.at[t], out_recv.at[t]) for t in range(ticks)]
    whole_link = [link(enc_made.at[t], enc_other.at[t]) for t in range(ticks - 1)]
    skip_link = [link(skips.at[t], skip_full.at[t, first]) for t in range(ticks)]
    dec_link = [link(made.at[t, final], dec_out.at[t]) for t in range(ticks)]
    back_input = link(dec_in, held.at[0, final])
    partial_link = [link(partial.at[t], partial.at[t]) for t in range(ticks)]
    scale_link = [link(scale.at[t], scale.at[t]) for t in range(ticks)]

    counter[0] = 0
    enc_load = local(enc_in, own_in.at[0])
    enter_load = [local(arrivals.at[t], own_in.at[t + 1]) for t in range(ticks - 1)]
    narrow_load = local(enc_w, narrow.at[:, :, pl.ds(0, part)])
    wide_load = local(dec_w, wide)
    enc_b_load = local(enc_b, bias.at[pl.ds(0, 1)])
    dec_b_load = local(dec_b, bias.at[pl.ds(8, 1)])
    dec_load = local(dec_in, held.at[0, first])
    skip_load = local(skips, skip_full.at[:, final])
    enc_store = [local(enc_final.at[t], enc_out.at[t]) for t in range(ticks)]
    dec_store = [local(made.at[t, first], dec_out.at[t]) for t in range(ticks)]

    for copy in (enc_load, narrow_load, enc_b_load, dec_b_load, wide_load):
        copy.start()

    @pl.when(is_dec)
    def _():
        dec_load.start()

    @pl.when(is_enc)
    def _():
        skip_load.start()

    @pl.when(s == 0)
    def _():
        for copy in enter_load:
            copy.start()

    barrier = pltpu.get_barrier_semaphore()

    def greet(segment, row):
        pl.semaphore_signal(
            barrier, inc=1, device_id={"segment": segment, "rows": row}, device_id_type=MESH
        )

    greet(s, 1 - r)

    @pl.when(s > 0)
    def _():
        greet(s - 1, r)

    @pl.when(s < last)
    def _():
        greet(s + 1, r)

    within = (s > 0) & (s < last)

    @pl.when(within)
    def _():
        pl.semaphore_wait(barrier, 3)

    @pl.when(jnp.logical_not(within))
    def _():
        pl.semaphore_wait(barrier, 2 if segments > 1 else 1)

    body = pl.ds(width, cells)

    def spread(value, span):
        column = lax.broadcasted_iota(jnp.int32, value.shape, 0) % width
        left = jnp.where(column == 0, 0.0, pltpu.roll(value, 1, 0))
        right = jnp.where(column == width - 1, 0.0, pltpu.roll(value, cells - 1, 0))
        columns[body, 0:span] = left.astype(jnp.bfloat16)
        columns[body, span : 2 * span] = value.astype(jnp.bfloat16)
        columns[body, 2 * span : 3 * span] = right.astype(jnp.bfloat16)

    def convolve(weights, span):
        def tap(d, carry):
            start = pl.multiple_of(d * width, width)
            total[...] += jnp.dot(
                columns[pl.ds(start, cells), 0 : 3 * span],
                weights[d].reshape(3 * span, channels),
                preferred_element_type=jnp.float32,
            )
            return carry

        total[...] = jnp.zeros_like(total)
        lax.fori_loop(0, taps, tap, 0)

    def skip_part(t):
        convolve(wide, channels)
        code, unit = coded(total[...])
        partial[t] = code
        scale[t] = jnp.broadcast_to(unit, scale.shape[1:])
        partial_link[t].start()
        scale_link[t].start()

    def image(ref):
        return ref[...].reshape(-1, channels).astype(jnp.float32)

    def whole(t):
        here = unpacked(enc_made[t].astype(jnp.float32), r)
        there = unpacked(enc_other[t].astype(jnp.float32), 1 - r)
        keep = low_lanes((own, channels), part) == (r == 0)
        for number in range(2):
            flat[pl.ds(number * own, own)] = jnp.where(keep, here[number], there[number])

    def cut(t):
        cut_send[t] = packed(image(own_in.at[t]), 1 - r).astype(jnp.bfloat16)
        cut_link[t].start()

    def enter(t):
        value = image(own_in.at[t])
        here = jnp.where(r == 0, value, pltpu.roll(value, part, 1))
        there = jnp.concatenate(unpacked(cut_recv[t].astype(jnp.float32), 0), axis=0)
        flat[pl.ds(0, own)] = jnp.where(r == 0, here, there)
        flat[pl.ds(own, own)] = jnp.where(r == 0, there, here)

    def enc_sums(t):
        if t == 0:
            cut_link[0].wait_recv()
            enter(0)
        else:

            @pl.when(s == 0)
            def _():
                enter_wait(t)
                enter(t)

            @pl.when(s > 0)
            def _():
                enc_relay(t - 1).wait_recv()
                upper, lower = unpacked(enc_held[t].astype(jnp.float32), 0)
                flat[pl.ds(0, own)] = upper
                flat[pl.ds(own, own)] = lower

        value = flat[:, 0:slot]
        spread(jnp.where(low_lanes(value.shape, part), value, 0.0), slot)
        convolve(narrow, slot)
        sums = total[...]
        code, unit = coded(packed(sums, 1 - r))
        sum_send[t] = code
        sum_scale_send[t] = jnp.broadcast_to(unit, sum_scale_send.shape[1:])
        sum_link[t].start()
        sum_scale_link[t].start()
        mine[...] = packed(sums, r)

    def enter_wait(t):
        cut_link[t].wait_recv()

    def enc_finish(t):
        line = jnp.broadcast_to(bias[0:1], (8, channels))
        turned = pltpu.roll(line, part, 1)
        low = low_lanes(line.shape, part)
        line = jnp.where(low == (r == 0), line, turned)[0:1]
        sum_scale_link[t].wait_recv()
        sum_link[t].wait_recv()
        value = mine[...] + decoded(sum_recv[t], sum_scale_recv[t, 0:1, 0:1]) + line
        result = silu(value).astype(jnp.bfloat16)
        enc_made[t] = result
        if t + 1 < ticks:

            @pl.when(s < last)
            def _():
                enc_relay(t).start()

            @pl.when(s == last)
            def _():
                whole_link[t].start()

            for segment in sorted({seg for _, e, seg in fresh if e == t and seg < last}):

                @pl.when(is_dec & (s == segment))
                def _():
                    whole_link[t].start()

        out_send[t] = packed(result.astype(jnp.float32), 1 - r).astype(jnp.bfloat16)
        out_link[t].start()

    def enc_store_rows(t):
        out_link[t].wait_recv()
        value = enc_made[t].astype(jnp.float32)
        upper = low_lanes(value.shape, part)
        there = jnp.concatenate(unpacked(out_recv[t].astype(jnp.float32), 1 - r), axis=0)
        enc_final[t] = (
            jnp.where(upper == (r == 0), value, there)
            .astype(jnp.bfloat16)
            .reshape(half, width, channels)
        )
        enc_store[t].start()

    fresh = [
        (t, e, segments - (t - e + 1) // 2)
        for t in range(ticks)
        for e in range(t)
        if (t - e) % 2 == 1 and segments >= (t - e + 1) // 2
    ]

    enc_load.wait()
    cut(0)

    @pl.when(is_dec)
    def _():
        for t in range(min(2, ticks)):
            skip_link[t].start()

    @pl.when(is_enc)
    def _():
        back_input.start()

    @pl.when(s == 0)
    def _():
        for copy in enter_load:
            copy.wait()
        for t in range(1, ticks):
            cut(t)

    edge = jnp.zeros((width, 3 * channels), jnp.bfloat16)
    columns[0:width] = edge
    columns[width + cells :] = edge
    for copy in (narrow_load, enc_b_load, dec_b_load, wide_load):
        copy.wait()
    if slot > part:
        narrow[:, :, part:] = jnp.zeros((taps, 3, slot - part, channels), jnp.bfloat16)

    @pl.when(is_dec)
    def _():
        dec_load.wait()

        def layer(t):
            if t == 0:
                back_input.wait_recv()
            else:

                @pl.when(s < last)
                def _():
                    dec_relay(t - 1).wait_recv()

                @pl.when(s == last)
                def _():
                    whole_link[t - 1].wait_recv()
                    whole(t - 1)
                    held[t] = flat[...].astype(jnp.bfloat16).reshape(rows, width, channels)

            spread(image(held.at[t]), channels)
            convolve(wide, channels)
            scale_link[t].wait_recv()
            partial_link[t].wait_recv()
            value = total[...] + decoded(partial[t], scale[t, 0:1, 0:1]) + bias[8:9]
            made[t] = silu(value).astype(jnp.bfloat16).reshape(rows, width, channels)
            if t + 1 < ticks:

                @pl.when(s > 0)
                def _():
                    dec_relay(t).start()

            dec_link[t].start()
            dec_store[t].start()

        for t in range(ticks):
            enc_sums(t)
            if t + 2 < ticks:
                skip_link[t + 2].start()
            if t > 0:
                layer(t - 1)
            enc_finish(t)
            if t > 0:
                enc_store_rows(t - 1)
        layer(ticks - 1)
        enc_store_rows(ticks - 1)
        for t in range(ticks):
            skip_link[t].wait_send()
            dec_link[t].wait_send()
            dec_store[t].wait()

        @pl.when(s > 0)
        def _():
            for t in range(ticks - 1):
                dec_relay(t).wait_send()

        for earlier, segment in sorted({(e, seg) for _, e, seg in fresh if seg < last}):

            @pl.when(s == segment)
            def _():
                whole_link[earlier].wait_send()

    @pl.when(is_enc)
    def _():
        skip_load.wait()

        def buffered(t):
            skip_link[t].wait_recv()
            usual = s >= 0
            for tick, _, segment in fresh:
                if tick == t:
                    usual = jnp.logical_and(usual, s != segment)

            @pl.when(usual)
            def _():
                spread(image(skip_full.at[t]), channels)
                skip_part(t)

        for t in range(ticks):
            enc_sums(t)
            buffered(t)
            enc_finish(t)
            for tick, earlier, segment in fresh:
                if earlier == t:

                    @pl.when(s == segment)
                    def _():
                        if tick == earlier + 1 or segment < last:
                            whole_link[t].wait_recv()
                        whole(t)
                        spread(flat[...], channels)
                        skip_part(tick)

            if t > 0:
                enc_store_rows(t - 1)
        enc_store_rows(ticks - 1)
        back_input.wait_send()
        for t in range(ticks):
            partial_link[t].wait_send()
            scale_link[t].wait_send()
            dec_link[t].wait_recv()

    cut_link[0].wait_send()
    for t in range(ticks):
        sum_link[t].wait_send()
        sum_scale_link[t].wait_send()
        out_link[t].wait_send()
        enc_store[t].wait()

    @pl.when(s == 0)
    def _():
        for t in range(1, ticks):
            cut_link[t].wait_send()

    @pl.when(s < last)
    def _():
        for t in range(ticks - 1):
            enc_relay(t).wait_send()

    @pl.when(s == last)
    def _():
        for t in range(ticks - 1):
            whole_link[t].wait_send()


def owned_shards(
    encoder_weight,
    encoder_bias,
    decoder_weight,
    decoder_bias,
    encoder_inputs,
    decoder_inputs,
    arrivals,
    skip_buffer,
):
    _, ticks, batch, half, width, channels = skip_buffer.shape
    taps, part = encoder_weight.shape[1], encoder_weight.shape[3]
    rows, own = 2 * half, half * width
    cells = 2 * own
    links = 9 * ticks + 9 * ticks
    slot = -(-part // 128) * 128
    anywhere = pl.BlockSpec(memory_space=pl.ANY)
    main = pl.BlockSpec(memory_space=pltpu.HBM)
    out = jax.ShapeDtypeStruct((ticks, half, width, channels), jnp.bfloat16)
    image = (ticks, rows, width, channels)

    def brief(*shape):
        return pltpu.VMEM(shape, jnp.bfloat16)

    def full(*shape):
        return pltpu.VMEM(shape, jnp.float32)

    encoder_made, decoder_made = pl.pallas_call(
        functools.partial(relay_kernel, lax.axis_size("segment")),
        out_shape=(out, out),
        in_specs=[main] * 8,
        out_specs=(anywhere, anywhere),
        scratch_shapes=[
            brief(taps, 3, channels, channels),
            brief(taps, 3, slot, channels),
            full(16, channels),
            brief(*image),
            brief(*image),
            brief(*image),
            brief(ticks, cells, channels),
            full(ticks, 8, 128),
            brief(ticks, half, width, channels),
            brief(ticks, own // 2, channels),
            brief(ticks, own // 2, channels),
            brief(ticks, own, channels),
            brief(ticks, own, channels),
            full(ticks, 8, 128),
            full(ticks, 8, 128),
            brief(ticks, own, channels),
            brief(ticks, own, channels),
            brief(ticks, own, channels),
            brief(ticks, own // 2, channels),
            brief(ticks, own // 2, channels),
            brief(ticks, half, width, channels),
            brief(cells + 2 * width, 3 * channels),
            full(cells, channels),
            full(own, channels),
            full(cells, channels),
            pltpu.SemaphoreType.DMA((10 + 4 * ticks,)),
            pltpu.SemaphoreType.DMA((links,)),
            pltpu.SemaphoreType.DMA((links,)),
            pltpu.SemaphoreType.DMA((2 * ticks,)),
            pltpu.SemaphoreType.DMA((2 * ticks,)),
        ],
        compiler_params=pltpu.CompilerParams(
            collective_id=0, has_side_effects=True, vmem_limit_bytes=40 * 1024 * 1024
        ),
    )(
        encoder_weight[0],
        encoder_bias,
        decoder_weight[0],
        decoder_bias,
        encoder_inputs[0, 0],
        decoder_inputs[0, 0],
        arrivals[:, 0],
        skip_buffer[0, :, 0],
    )
    return encoder_made[None, :, None], decoder_made[None, :, None]


def gathered_shards(
    encoder_weight,
    encoder_bias,
    decoder_weight,
    decoder_bias,
    encoder_inputs,
    decoder_inputs,
    arrivals,
    skip_buffer,
):
    segment_count = lax.axis_size("segment")
    segment_index = lax.axis_index("segment")
    rows_local = encoder_inputs.shape[2]
    total_rows = rows_local * lax.axis_size("rows")
    first_row = lax.axis_index("rows") * rows_local
    channels = encoder_weight.shape[4]
    tick_count = skip_buffer.shape[1]
    skip_lag = 2 * (segment_count - segment_index) - 1
    margin = 2
    paired = decoder_weight.reshape(1, 3, 3, decoder_weight.shape[3] // 2, 2 * channels)
    encoder_offset = encoder_bias[0]
    decoder_offset = decoder_bias[0]
    kernels = [None, None]
    gathered = (
        lax.all_gather(encoder_weight, "rows", axis=3, tiled=True),
        lax.all_gather(paired, "rows", axis=3, tiled=True),
    )
    kernels[0] = gathered[0][0]
    kernels[1] = gathered[1].reshape(3, 3, 2 * channels, channels)
    encoder_now = encoder_inputs[0]
    decoder_now = decoder_inputs[0]
    arrival_state = [(arrivals[number], 0) for number in range(tick_count - 1)]
    skip_state = [(skip_buffer[0, number], 0) for number in range(tick_count)]
    encoder_made = []
    encoder_cores = []
    decoder_cores = []

    def pick_skip(period, want_rim):
        base_skip, base_rim = skip_state[period]
        chosen = trim_rows(base_skip, base_rim, want_rim)
        for earlier in range(period):
            if (period - earlier) % 2 == 1:
                made_value, made_rim = encoder_made[earlier]
                chosen = jnp.where(
                    skip_lag == period - earlier, trim_rows(made_value, made_rim, want_rim), chosen
                )
        return chosen

    for period in range(tick_count):
        position = period % margin
        rim_before = margin - position
        if position == 0:
            skip_now = pick_skip(period, 0)
            pieces = [encoder_now, decoder_now, skip_now]
            pieces = pieces + [arrival_state[period][0], skip_state[period + 1][0]]
            joined = jnp.concatenate(pieces, axis=3)
            rimmed = padded(joined, (("rows", 1),), margin)
            sections = [
                rimmed[..., number * channels : (number + 1) * channels]
                for number in range(len(pieces))
            ]
            encoder_now = sections[0]
            decoder_now = sections[1]
            skip_now = sections[2]
            arrival_state[period] = (sections[3], margin)
            skip_state[period + 1] = (sections[4], margin)
        else:
            skip_now = pick_skip(period, rim_before)
        rim_after = rim_before - 1
        decoder_source = jnp.concatenate([decoder_now, skip_now], axis=3)
        encoder_out = finish(
            channel_part(encoder_now, kernels[0]), encoder_offset, rim_after, first_row, total_rows
        )
        decoder_out = finish(
            channel_part(decoder_source, kernels[1]),
            decoder_offset,
            rim_after,
            first_row,
            total_rows,
        )
        encoder_made.append((encoder_out, rim_after))
        encoder_cores.append(trim_rows(encoder_out, rim_after, 0))
        decoder_cores.append(trim_rows(decoder_out, rim_after, 0))
        if period + 1 < tick_count:
            encoder_moved = shifted(encoder_out, "segment", 1)
            decoder_moved = shifted(decoder_out, "segment", -1)
            arrival, arrival_rim = arrival_state[period]
            encoder_now = jnp.where(
                segment_index == 0, trim_rows(arrival, arrival_rim, rim_after), encoder_moved
            )
            decoder_now = jnp.where(segment_index == segment_count - 1, encoder_out, decoder_moved)
    return (jnp.stack(encoder_cores, axis=0)[None], jnp.stack(decoder_cores, axis=0)[None])


def solution(mesh):
    return jax.shard_map(
        owned_shards if mesh.shape["rows"] == 2 else gathered_shards,
        mesh=mesh,
        in_specs=(
            P("segment", None, None, "rows", None),
            P("segment", None),
            P("segment", None, None, "rows", None),
            P("segment", None),
            P("segment", None, "rows", None, None),
            P("segment", None, "rows", None, None),
            P(None, None, "rows", None, None),
            P("segment", None, None, "rows", None, None),
        ),
        out_specs=(
            P("segment", None, None, "rows", None, None),
            P("segment", None, None, "rows", None, None),
        ),
        check_vma=False,
    )
```

```python
import functools

import jax
import jax.numpy as jnp
from jax import lax
from jax.experimental import pallas as pl
from jax.experimental.pallas import tpu as pltpu
from jax.sharding import PartitionSpec as P

NUMBERS = ("NHWC", "HWIO", "NHWC")


def padded(value, sides, width):
    for axis, dim in sides:
        peers, length = (lax.axis_size(axis), value.shape[dim])
        up = [(i, (i + 1) % peers) for i in range(peers - 1)]
        down = [(j, i) for i, j in up]
        last = lax.slice_in_dim(value, length - width, length, axis=dim)
        initial = lax.slice_in_dim(value, 0, width, axis=dim)
        before = lax.ppermute(last, axis, up)
        after = lax.ppermute(initial, axis, down)
        value = jnp.concatenate([before, value, after], axis=dim)
    return value


def shifted(block, axis, distance):
    devices = range(lax.axis_size(axis))
    route = [(i - distance, i) for i in devices if i - distance in devices]
    return lax.ppermute(block, axis, route)


def channel_part(source, kernel):
    return lax.conv_general_dilated(
        source,
        kernel,
        (1, 1),
        ((0, 0), (1, 1)),
        dimension_numbers=NUMBERS,
        preferred_element_type=jnp.float32,
    )


def finish(result, offset, rim_after, first_row, total_rows):
    result = jax.nn.silu(result + offset)
    if rim_after > 0:
        global_row = first_row - rim_after + jnp.arange(result.shape[1])
        inside = (global_row >= 0) & (global_row < total_rows)
        result = jnp.where(inside[None, :, None, None], result, 0.0)
    return result.astype(jnp.bfloat16)


def trim_rows(source, have_rim, want_rim):
    excess = have_rim - want_rim
    if excess == 0:
        return source
    return source[:, excess : source.shape[1] - excess]


MESH = pl.DeviceIdType.MESH
SENT = jnp.bfloat16
TOP = 32768.0


def coded(found):
    top = jnp.maximum(jnp.max(jnp.abs(found), axis=(0, 1), keepdims=True), 1e-25)
    scaled = found * (TOP / top)
    power = scaled * scaled
    power = power * power
    power = power * power
    return jnp.where(scaled < 0.0, -power, power).astype(SENT), top * (1.0 / TOP)


def decoded(code, scale):
    power = code.astype(jnp.float32)
    root = jnp.sqrt(jnp.sqrt(jnp.sqrt(jnp.abs(power))))
    return jnp.where(power < 0.0, -root, root) * scale


def low_lanes(shape, part):
    return lax.broadcasted_iota(jnp.int32, shape, 1) < part


def packed(value, side):
    count, part = value.shape[0] // 2, value.shape[1] // 2
    upper, lower = value[:count], value[count:]
    left = jnp.where(side == 0, upper, pltpu.roll(upper, part, 1))
    right = jnp.where(side == 0, pltpu.roll(lower, part, 1), lower)
    return jnp.where(low_lanes(upper.shape, part), left, right)


def unpacked(value, side):
    part = value.shape[1] // 2
    turned = pltpu.roll(value, part, 1)
    return jnp.where(side == 0, value, turned), jnp.where(side == 0, turned, value)


def silu(value):
    return value / (1.0 + jnp.exp(-value))


def relay_kernel(
    segments,
    enc_w,
    enc_b,
    dec_w,
    dec_b,
    enc_in,
    dec_in,
    arrivals,
    skips,
    enc_out,
    dec_out,
    wide,
    narrow,
    bias,
    held,
    made,
    skip_full,
    partial,
    scale,
    own_in,
    cut_send,
    cut_recv,
    sum_send,
    sum_recv,
    sum_scale_send,
    sum_scale_recv,
    enc_held,
    enc_made,
    enc_other,
    out_send,
    out_recv,
    enc_final,
    columns,
    total,
    mine,
    flat,
    local_sem,
    link_send,
    link_recv,
    relay_send,
    relay_recv,
):
    s = lax.axis_index("segment")
    r = lax.axis_index("rows")
    ticks, half, width, channels = skips.shape
    rows = 2 * half
    cells = rows * width
    own = half * width
    taps = enc_w.shape[0]
    part = enc_w.shape[2]
    slot = narrow.shape[2]
    last = segments - 1
    is_enc = r == 1
    is_dec = r == 0
    counter = [0]

    def link(src, dst):
        number = counter[0]
        counter[0] = number + 1
        return pltpu.make_async_remote_copy(
            src_ref=src,
            dst_ref=dst,
            send_sem=link_send.at[number],
            recv_sem=link_recv.at[number],
            device_id={"segment": s, "rows": 1 - r},
            device_id_type=MESH,
        )

    def relay(number, src, dst, segment):
        return pltpu.make_async_remote_copy(
            src_ref=src,
            dst_ref=dst,
            send_sem=relay_send.at[number],
            recv_sem=relay_recv.at[number],
            device_id={"segment": segment, "rows": r},
            device_id_type=MESH,
        )

    def local(src, dst):
        number = counter[0]
        counter[0] = number + 1
        return pltpu.make_async_copy(src, dst, local_sem.at[number])

    def enc_relay(t):
        return relay(t, enc_made.at[t], enc_held.at[t + 1], s + 1)

    def dec_relay(t):
        return relay(ticks + t, made.at[t], held.at[t + 1], s - 1)

    first, final = pl.ds(0, half), pl.ds(half, half)

    cut_link = [link(cut_send.at[t], cut_recv.at[t]) for t in range(ticks)]
    sum_link = [link(sum_send.at[t], sum_recv.at[t]) for t in range(ticks)]
    sum_scale_link = [link(sum_scale_send.at[t], sum_scale_recv.at[t]) for t in range(ticks)]
    out_link = [link(out_send.at[t], out_recv.at[t]) for t in range(ticks)]
    whole_link = [link(enc_made.at[t], enc_other.at[t]) for t in range(ticks - 1)]
    skip_link = [link(skips.at[t], skip_full.at[t, first]) for t in range(ticks)]
    dec_link = [link(made.at[t, final], dec_out.at[t]) for t in range(ticks)]
    back_input = link(dec_in, held.at[0, final])
    partial_link = [link(partial.at[t], partial.at[t]) for t in range(ticks)]
    scale_link = [link(scale.at[t], scale.at[t]) for t in range(ticks)]

    counter[0] = 0
    enc_load = local(enc_in, own_in.at[0])
    enter_load = [local(arrivals.at[t], own_in.at[t + 1]) for t in range(ticks - 1)]
    narrow_load = local(enc_w, narrow.at[:, :, pl.ds(0, part)])
    wide_load = local(dec_w, wide)
    enc_b_load = local(enc_b, bias.at[pl.ds(0, 1)])
    dec_b_load = local(dec_b, bias.at[pl.ds(8, 1)])
    dec_load = local(dec_in, held.at[0, first])
    skip_load = local(skips, skip_full.at[:, final])
    enc_store = [local(enc_final.at[t], enc_out.at[t]) for t in range(ticks)]
    dec_store = [local(made.at[t, first], dec_out.at[t]) for t in range(ticks)]

    for copy in (enc_load, narrow_load, enc_b_load, dec_b_load, wide_load):
        copy.start()

    @pl.when(is_dec)
    def _():
        dec_load.start()

    @pl.when(is_enc)
    def _():
        skip_load.start()

    @pl.when(s == 0)
    def _():
        for copy in enter_load:
            copy.start()

    barrier = pltpu.get_barrier_semaphore()

    def greet(segment, row):
        pl.semaphore_signal(
            barrier, inc=1, device_id={"segment": segment, "rows": row}, device_id_type=MESH
        )

    greet(s, 1 - r)

    @pl.when(s > 0)
    def _():
        greet(s - 1, r)

    @pl.when(s < last)
    def _():
        greet(s + 1, r)

    within = (s > 0) & (s < last)

    @pl.when(within)
    def _():
        pl.semaphore_wait(barrier, 3)

    @pl.when(jnp.logical_not(within))
    def _():
        pl.semaphore_wait(barrier, 2 if segments > 1 else 1)

    body = pl.ds(width, cells)

    def spread(value, span):
        column = lax.broadcasted_iota(jnp.int32, value.shape, 0) % width
        left = jnp.where(column == 0, 0.0, pltpu.roll(value, 1, 0))
        right = jnp.where(column == width - 1, 0.0, pltpu.roll(value, cells - 1, 0))
        columns[body, 0:span] = left.astype(jnp.bfloat16)
        columns[body, span : 2 * span] = value.astype(jnp.bfloat16)
        columns[body, 2 * span : 3 * span] = right.astype(jnp.bfloat16)

    def convolve(weights, span):
        def tap(d, carry):
            start = pl.multiple_of(d * width, width)
            total[...] += jnp.dot(
                columns[pl.ds(start, cells), 0 : 3 * span],
                weights[d].reshape(3 * span, channels),
                preferred_element_type=jnp.float32,
            )
            return carry

        total[...] = jnp.zeros_like(total)
        lax.fori_loop(0, taps, tap, 0)

    def skip_part(t):
        convolve(wide, channels)
        code, unit = coded(total[...])
        partial[t] = code
        scale[t] = jnp.broadcast_to(unit, scale.shape[1:])
        partial_link[t].start()
        scale_link[t].start()

    def image(ref):
        return ref[...].reshape(-1, channels).astype(jnp.float32)

    def whole(t):
        here = unpacked(enc_made[t].astype(jnp.float32), r)
        there = unpacked(enc_other[t].astype(jnp.float32), 1 - r)
        keep = low_lanes((own, channels), part) == (r == 0)
        for number in range(2):
            flat[pl.ds(number * own, own)] = jnp.where(keep, here[number], there[number])

    def cut(t):
        cut_send[t] = packed(image(own_in.at[t]), 1 - r).astype(jnp.bfloat16)
        cut_link[t].start()

    def enter(t):
        value = image(own_in.at[t])
        here = jnp.where(r == 0, value, pltpu.roll(value, part, 1))
        there = jnp.concatenate(unpacked(cut_recv[t].astype(jnp.float32), 0), axis=0)
        flat[pl.ds(0, own)] = jnp.where(r == 0, here, there)
        flat[pl.ds(own, own)] = jnp.where(r == 0, there, here)

    def enc_sums(t):
        if t == 0:
            cut_link[0].wait_recv()
            enter(0)
        else:

            @pl.when(s == 0)
            def _():
                enter_wait(t)
                enter(t)

            @pl.when(s > 0)
            def _():
                enc_relay(t - 1).wait_recv()
                upper, lower = unpacked(enc_held[t].astype(jnp.float32), 0)
                flat[pl.ds(0, own)] = upper
                flat[pl.ds(own, own)] = lower

        value = flat[:, 0:slot]
        spread(jnp.where(low_lanes(value.shape, part), value, 0.0), slot)
        convolve(narrow, slot)
        sums = total[...]
        code, unit = coded(packed(sums, 1 - r))
        sum_send[t] = code
        sum_scale_send[t] = jnp.broadcast_to(unit, sum_scale_send.shape[1:])
        sum_link[t].start()
        sum_scale_link[t].start()
        mine[...] = packed(sums, r)

    def enter_wait(t):
        cut_link[t].wait_recv()

    def enc_finish(t):
        line = jnp.broadcast_to(bias[0:1], (8, channels))
        turned = pltpu.roll(line, part, 1)
        low = low_lanes(line.shape, part)
        line = jnp.where(low == (r == 0), line, turned)[0:1]
        sum_scale_link[t].wait_recv()
        sum_link[t].wait_recv()
        value = mine[...] + decoded(sum_recv[t], sum_scale_recv[t, 0:1, 0:1]) + line
        result = silu(value).astype(jnp.bfloat16)
        enc_made[t] = result
        if t + 1 < ticks:

            @pl.when(s < last)
            def _():
                enc_relay(t).start()

            @pl.when(s == last)
            def _():
                whole_link[t].start()

            for segment in sorted({seg for _, e, seg in fresh if e == t and seg < last}):

                @pl.when(is_dec & (s == segment))
                def _():
                    whole_link[t].start()

        out_send[t] = packed(result.astype(jnp.float32), 1 - r).astype(jnp.bfloat16)
        out_link[t].start()

    def enc_store_rows(t):
        out_link[t].wait_recv()
        value = enc_made[t].astype(jnp.float32)
        upper = low_lanes(value.shape, part)
        there = jnp.concatenate(unpacked(out_recv[t].astype(jnp.float32), 1 - r), axis=0)
        enc_final[t] = (
            jnp.where(upper == (r == 0), value, there)
            .astype(jnp.bfloat16)
            .reshape(half, width, channels)
        )
        enc_store[t].start()

    fresh = [
        (t, e, segments - (t - e + 1) // 2)
        for t in range(ticks)
        for e in range(t)
        if (t - e) % 2 == 1 and segments >= (t - e + 1) // 2
    ]

    enc_load.wait()
    cut(0)

    @pl.when(is_dec)
    def _():
        for t in range(min(2, ticks)):
            skip_link[t].start()

    @pl.when(is_enc)
    def _():
        back_input.start()

    @pl.when(s == 0)
    def _():
        for copy in enter_load:
            copy.wait()
        for t in range(1, ticks):
            cut(t)

    edge = jnp.zeros((width, 3 * channels), jnp.bfloat16)
    columns[0:width] = edge
    columns[width + cells :] = edge
    for copy in (narrow_load, enc_b_load, dec_b_load, wide_load):
        copy.wait()
    if slot > part:
        narrow[:, :, part:] = jnp.zeros((taps, 3, slot - part, channels), jnp.bfloat16)

    @pl.when(is_dec)
    def _():
        dec_load.wait()

        def layer(t):
            if t == 0:
                back_input.wait_recv()
            else:

                @pl.when(s < last)
                def _():
                    dec_relay(t - 1).wait_recv()

                @pl.when(s == last)
                def _():
                    whole_link[t - 1].wait_recv()
                    whole(t - 1)
                    held[t] = flat[...].astype(jnp.bfloat16).reshape(rows, width, channels)

            spread(image(held.at[t]), channels)
            convolve(wide, channels)
            scale_link[t].wait_recv()
            partial_link[t].wait_recv()
            value = total[...] + decoded(partial[t], scale[t, 0:1, 0:1]) + bias[8:9]
            made[t] = silu(value).astype(jnp.bfloat16).reshape(rows, width, channels)
            if t + 1 < ticks:

                @pl.when(s > 0)
                def _():
                    dec_relay(t).start()

            dec_link[t].start()
            dec_store[t].start()

        for t in range(ticks):
            enc_sums(t)
            if t + 2 < ticks:
                skip_link[t + 2].start()
            if t > 0:
                layer(t - 1)
            enc_finish(t)
            if t > 0:
                enc_store_rows(t - 1)
        layer(ticks - 1)
        enc_store_rows(ticks - 1)
        for t in range(ticks):
            skip_link[t].wait_send()
            dec_link[t].wait_send()
            dec_store[t].wait()

        @pl.when(s > 0)
        def _():
            for t in range(ticks - 1):
                dec_relay(t).wait_send()

        for earlier, segment in sorted({(e, seg) for _, e, seg in fresh if seg < last}):

            @pl.when(s == segment)
            def _():
                whole_link[earlier].wait_send()

    @pl.when(is_enc)
    def _():
        skip_load.wait()

        def buffered(t):
            skip_link[t].wait_recv()
            usual = s >= 0
            for tick, _, segment in fresh:
                if tick == t:
                    usual = jnp.logical_and(usual, s != segment)

            @pl.when(usual)
            def _():
                spread(image(skip_full.at[t]), channels)
                skip_part(t)

        for t in range(ticks):
            enc_sums(t)
            buffered(t)
            enc_finish(t)
            for tick, earlier, segment in fresh:
                if earlier == t:

                    @pl.when(s == segment)
                    def _():
                        if tick == earlier + 1 or segment < last:
                            whole_link[t].wait_recv()
                        whole(t)
                        spread(flat[...], channels)
                        skip_part(tick)

            if t > 0:
                enc_store_rows(t - 1)
        enc_store_rows(ticks - 1)
        back_input.wait_send()
        for t in range(ticks):
            partial_link[t].wait_send()
            scale_link[t].wait_send()
            dec_link[t].wait_recv()

    cut_link[0].wait_send()
    for t in range(ticks):
        sum_link[t].wait_send()
        sum_scale_link[t].wait_send()
        out_link[t].wait_send()
        enc_store[t].wait()

    @pl.when(s == 0)
    def _():
        for t in range(1, ticks):
            cut_link[t].wait_send()

    @pl.when(s < last)
    def _():
        for t in range(ticks - 1):
            enc_relay(t).wait_send()

    @pl.when(s == last)
    def _():
        for t in range(ticks - 1):
            whole_link[t].wait_send()


def owned_shards(
    encoder_weight,
    encoder_bias,
    decoder_weight,
    decoder_bias,
    encoder_inputs,
    decoder_inputs,
    arrivals,
    skip_buffer,
):
    _, ticks, batch, half, width, channels = skip_buffer.shape
    taps, part = encoder_weight.shape[1], encoder_weight.shape[3]
    rows, own = 2 * half, half * width
    cells = 2 * own
    links = 9 * ticks + 9 * ticks
    slot = -(-part // 128) * 128
    anywhere = pl.BlockSpec(memory_space=pl.ANY)
    main = pl.BlockSpec(memory_space=pltpu.HBM)
    out = jax.ShapeDtypeStruct((ticks, half, width, channels), jnp.bfloat16)
    image = (ticks, rows, width, channels)

    def brief(*shape):
        return pltpu.VMEM(shape, jnp.bfloat16)

    def full(*shape):
        return pltpu.VMEM(shape, jnp.float32)

    encoder_made, decoder_made = pl.pallas_call(
        functools.partial(relay_kernel, lax.axis_size("segment")),
        out_shape=(out, out),
        in_specs=[main] * 8,
        out_specs=(anywhere, anywhere),
        scratch_shapes=[
            brief(taps, 3, channels, channels),
            brief(taps, 3, slot, channels),
            full(16, channels),
            brief(*image),
            brief(*image),
            brief(*image),
            brief(ticks, cells, channels),
            full(ticks, 8, 128),
            brief(ticks, half, width, channels),
            brief(ticks, own // 2, channels),
            brief(ticks, own // 2, channels),
            brief(ticks, own, channels),
            brief(ticks, own, channels),
            full(ticks, 8, 128),
            full(ticks, 8, 128),
            brief(ticks, own, channels),
            brief(ticks, own, channels),
            brief(ticks, own, channels),
            brief(ticks, own // 2, channels),
            brief(ticks, own // 2, channels),
            brief(ticks, half, width, channels),
            brief(cells + 2 * width, 3 * channels),
            full(cells, channels),
            full(own, channels),
            full(cells, channels),
            pltpu.SemaphoreType.DMA((10 + 4 * ticks,)),
            pltpu.SemaphoreType.DMA((links,)),
            pltpu.SemaphoreType.DMA((links,)),
            pltpu.SemaphoreType.DMA((2 * ticks,)),
            pltpu.SemaphoreType.DMA((2 * ticks,)),
        ],
        compiler_params=pltpu.CompilerParams(
            collective_id=0, has_side_effects=True, vmem_limit_bytes=63 * 1024 * 1024
        ),
    )(
        encoder_weight[0],
        encoder_bias,
        decoder_weight[0],
        decoder_bias,
        encoder_inputs[0, 0],
        decoder_inputs[0, 0],
        arrivals[:, 0],
        skip_buffer[0, :, 0],
    )
    return encoder_made[None, :, None], decoder_made[None, :, None]


def gathered_shards(
    encoder_weight,
    encoder_bias,
    decoder_weight,
    decoder_bias,
    encoder_inputs,
    decoder_inputs,
    arrivals,
    skip_buffer,
):
    segment_count = lax.axis_size("segment")
    segment_index = lax.axis_index("segment")
    rows_local = encoder_inputs.shape[2]
    total_rows = rows_local * lax.axis_size("rows")
    first_row = lax.axis_index("rows") * rows_local
    channels = encoder_weight.shape[4]
    tick_count = skip_buffer.shape[1]
    skip_lag = 2 * (segment_count - segment_index) - 1
    margin = 2
    paired = decoder_weight.reshape(1, 3, 3, decoder_weight.shape[3] // 2, 2 * channels)
    encoder_offset = encoder_bias[0]
    decoder_offset = decoder_bias[0]
    kernels = [None, None]
    gathered = (
        lax.all_gather(encoder_weight, "rows", axis=3, tiled=True),
        lax.all_gather(paired, "rows", axis=3, tiled=True),
    )
    kernels[0] = gathered[0][0]
    kernels[1] = gathered[1].reshape(3, 3, 2 * channels, channels)
    encoder_now = encoder_inputs[0]
    decoder_now = decoder_inputs[0]
    arrival_state = [(arrivals[number], 0) for number in range(tick_count - 1)]
    skip_state = [(skip_buffer[0, number], 0) for number in range(tick_count)]
    encoder_made = []
    encoder_cores = []
    decoder_cores = []

    def pick_skip(period, want_rim):
        base_skip, base_rim = skip_state[period]
        chosen = trim_rows(base_skip, base_rim, want_rim)
        for earlier in range(period):
            if (period - earlier) % 2 == 1:
                made_value, made_rim = encoder_made[earlier]
                chosen = jnp.where(
                    skip_lag == period - earlier, trim_rows(made_value, made_rim, want_rim), chosen
                )
        return chosen

    for period in range(tick_count):
        position = period % margin
        rim_before = margin - position
        if position == 0:
            skip_now = pick_skip(period, 0)
            pieces = [encoder_now, decoder_now, skip_now]
            pieces = pieces + [arrival_state[period][0], skip_state[period + 1][0]]
            joined = jnp.concatenate(pieces, axis=3)
            rimmed = padded(joined, (("rows", 1),), margin)
            sections = [
                rimmed[..., number * channels : (number + 1) * channels]
                for number in range(len(pieces))
            ]
            encoder_now = sections[0]
            decoder_now = sections[1]
            skip_now = sections[2]
            arrival_state[period] = (sections[3], margin)
            skip_state[period + 1] = (sections[4], margin)
        else:
            skip_now = pick_skip(period, rim_before)
        rim_after = rim_before - 1
        decoder_source = jnp.concatenate([decoder_now, skip_now], axis=3)
        encoder_out = finish(
            channel_part(encoder_now, kernels[0]), encoder_offset, rim_after, first_row, total_rows
        )
        decoder_out = finish(
            channel_part(decoder_source, kernels[1]),
            decoder_offset,
            rim_after,
            first_row,
            total_rows,
        )
        encoder_made.append((encoder_out, rim_after))
        encoder_cores.append(trim_rows(encoder_out, rim_after, 0))
        decoder_cores.append(trim_rows(decoder_out, rim_after, 0))
        if period + 1 < tick_count:
            encoder_moved = shifted(encoder_out, "segment", 1)
            decoder_moved = shifted(decoder_out, "segment", -1)
            arrival, arrival_rim = arrival_state[period]
            encoder_now = jnp.where(
                segment_index == 0, trim_rows(arrival, arrival_rim, rim_after), encoder_moved
            )
            decoder_now = jnp.where(segment_index == segment_count - 1, encoder_out, decoder_moved)
    return (jnp.stack(encoder_cores, axis=0)[None], jnp.stack(decoder_cores, axis=0)[None])


def solution(mesh):
    return jax.shard_map(
        owned_shards if mesh.shape["rows"] == 2 else gathered_shards,
        mesh=mesh,
        in_specs=(
            P("segment", None, None, "rows", None),
            P("segment", None),
            P("segment", None, None, "rows", None),
            P("segment", None),
            P("segment", None, "rows", None, None),
            P("segment", None, "rows", None, None),
            P(None, None, "rows", None, None),
            P("segment", None, None, "rows", None, None),
        ),
        out_specs=(
            P("segment", None, None, "rows", None, None),
            P("segment", None, None, "rows", None, None),
        ),
        check_vma=False,
    )
```
